32 devices in a mesh: row: 4 (over z), col: 4 (over x, core), pair: 2 (over y).
Axes of the slice: x: 2, y: 2, z: 4, core: 2. Of those that a mesh axis runs over, the one named last changes fastest.
Arguments:
- pair_slab: bfloat16 [768, 16384], P('pair', 'row'), may hold values from -0.875 to 0.875
- pair_weights: float32 [768], P('pair'), may hold values from 0.2 to 2
Outputs:
- polarizability: float32 [16384, 16384], P('row', ('col', 'pair'))
The draws below stay inside these ranges and needn't reach their ends.
All inputs are finite; a program needn't handle non-finite values.
Results may differ from the reference program's by a relative error of at most 0.0085.
Values may be sent and summed in bfloat16 or wider, within the bound.
No kernel may reach another device: no remote copies, remote signals or barrier semaphores. Data moves between devices by JAX's collectives and lax.ppermute only.
A program may use at most 128 MiB of HBM per device.

```python
import math
import jax
import jax.numpy as jnp
from jax import lax

NAUX = 16384
NPAIR = 768


def shard_levels(stream_key, shape, cuts, low, high):
    loudness, own = 1.0, jax.random.fold_in(stream_key, 6)
    for position, blocks in cuts:
        steps = jnp.exp(jax.random.uniform(jax.random.fold_in(own, position), (blocks,), jnp.float32, low / len(cuts), high / len(cuts)))
        loudness = loudness * jnp.repeat(steps, shape[position] // blocks).reshape([-1 if axis == position else 1 for axis in range(len(shape))])
    return loudness


def normal_values(stream_key, shape, deviation, bound, cuts=(), kind=jnp.bfloat16):
    factor_of = shard_levels(stream_key, shape, cuts, -0.22, 0.18) if cuts else 1.0
    result = jax.random.normal(stream_key, shape, jnp.float32) * deviation * factor_of
    return jnp.minimum(jnp.maximum(result, -bound), bound).astype(kind)


def setup_inputs(seed: int = 0) -> dict:
    key_of = jax.random.split(jax.random.key(seed), 3)
    pair_slab = normal_values(key_of[0], (NPAIR, NAUX), (NPAIR // 16) ** -0.5, 0.875, ((0, 2), (1, 4)))
    pair_weights = jnp.clip(jnp.exp(math.log(2.0) - 2.3025851 * jax.random.uniform(key_of[1], (NPAIR,), jnp.float32) ** shard_levels(key_of[1], (NPAIR,), ((0, 2),), -0.2, 0.2)), 0.2, 2.0)
    return {"pair_slab": pair_slab, "pair_weights": pair_weights}


def reference(pair_slab, pair_weights):
    weighted = (pair_weights[:, None] * pair_slab.astype(jnp.float32)).astype(jnp.bfloat16)
    return lax.dot_general(weighted.astype(jnp.float32), pair_slab.astype(jnp.float32), (((0,), (0,)), ((), ())), precision=lax.Precision.HIGHEST, preferred_element_type=jnp.float32)
```

```python
import jax
import jax.numpy as jnp
from jax import lax
from jax.experimental import pallas as pl
from jax.experimental.pallas import tpu as pltpu
from jax.sharding import PartitionSpec as P

AXES = ("row", "col", "pair")


def dot_over_pairs(left, right):
    return lax.dot_general(
        left, right, (((0,), (0,)), ((), ())), preferred_element_type=jnp.float32
    )


def product_kernel(own_rows, other_rows, own_cols, other_cols, *refs):
    out = refs[-1]
    out[...] = dot_over_pairs(own_rows[...], own_cols[...]) + dot_over_pairs(
        other_rows[...], other_cols[...]
    )


def product(own_rows, other_rows, own_cols, other_cols, result, place, columns):
    own, rows = own_rows.shape
    other, width = other_cols.shape
    tile = 1024 if rows % 1024 == 0 else rows
    in_specs = [
        pl.BlockSpec((own, tile), lambda i: (0, i)),
        pl.BlockSpec((other, tile), lambda i: (0, i)),
        pl.BlockSpec((own, width), lambda i: (0, 0)),
        pl.BlockSpec((other, width), lambda i: (0, 0)),
    ]
    args = [own_rows, other_rows, own_cols, other_cols]
    aliases = {}
    if result is not None:
        in_specs.append(pl.BlockSpec(memory_space=pl.ANY))
        args.append(result)
        aliases = {4: 0}
    return pl.pallas_call(
        product_kernel,
        grid=(rows // tile,),
        in_specs=in_specs,
        out_specs=pl.BlockSpec((tile, width), lambda i: (i, place)),
        out_shape=jax.ShapeDtypeStruct((rows, columns), jnp.float32),
        input_output_aliases=aliases,
        compiler_params=pltpu.CompilerParams(vmem_limit_bytes=40 * 2**20),
        cost_estimate=pl.CostEstimate(
            flops=2 * rows * width * (own + other),
            bytes_accessed=4 * rows * width + 2 * rows * (own + other),
            transcendentals=0,
        ),
    )(*args)


def solution(mesh):
    R, C, Q = (mesh.shape[axis] for axis in AXES)

    def number(r, c, p):
        return (r * C + c) * Q + p

    def permute(block, route):
        pairs = []
        for r in range(R):
            for c in range(C):
                for p in range(Q):
                    target = route(r, c, p)
                    if target is not None and 0 <= target[0] < R:
                        pairs.append((number(r, c, p), number(*target)))
        return lax.ppermute(block, AXES, pairs) if pairs else jnp.zeros_like(block)

    def spread(block, carried):
        step = permute(block, lambda r, c, p: (r - 1, c, p) if r == carried[c] else None)
        step = step + permute(block, lambda r, c, p: (r + 1, c, p) if r == carried[c] else None)
        total = step
        for hop in range(1, R - 1):

            def onward(r, c, p):
                way = r - carried[c]
                if abs(way) != hop:
                    return None
                return (r + 1, c, p) if way > 0 else (r - 1, c, p)

            step = permute(step, onward)
            total = total + step
        return total

    def cross(block, carried):
        return permute(
            block,
            lambda r, c, p: (r, carried[c], p) if carried[c] not in (c, r) else None,
        )

    def on_device(slab, weights):
        pairs, block = slab.shape
        width = block // Q
        half = width // 2
        r, c, p = (lax.axis_index(axis) for axis in AXES)
        core = c % 2
        mirrored = [C - 1 - i for i in range(C)]
        native = list(range(C))
        edges = [C - 1 - i if i in (0, C - 1) else i for i in range(C)]

        def columns_of(array, start, size):
            return lax.dynamic_slice_in_dim(array, start, size, 1)

        own0 = columns_of(slab, p * width, half)
        own1 = columns_of(slab, p * width + half, half)

        def exchange(shift, relative, offset, size):
            start = (p - shift + relative) % Q * width + offset
            mine = lax.dynamic_slice(slab, (core * (pairs // 2), start), (pairs // 2, size))
            mine = permute(mine, lambda r, c, p: (r, c, (p - shift) % Q))
            theirs = permute(mine, lambda r, c, p: (r, c ^ 1, p))
            return jnp.concatenate(
                [jnp.where(core == 0, mine, theirs), jnp.where(core == 0, theirs, mine)], 0
            )

        shifts = range(1, Q)
        other0 = jnp.concatenate([exchange(s, 0, 0, half) for s in shifts], 0)
        other1 = jnp.concatenate([exchange(s, 0, half, half) for s in shifts], 0)
        rest = [
            jnp.concatenate([exchange(s, j, 0, width) for s in shifts], 0) for j in range(1, Q)
        ]
        other_weights = jnp.concatenate(
            [permute(weights, lambda r, c, p: (r, c, (p - s) % Q)) for s in shifts]
        )

        def taken(carried, block):
            got = spread(block, carried)
            if carried == native:
                return jnp.where(r == c, block, got)
            crossed = cross(got, carried)
            away = jnp.zeros((), bool)
            for i in range(C):
                if carried[i] != i:
                    away = away | (c == i)
            return jnp.where(r == c, block, jnp.where(away, crossed, got))

        cols_own0 = taken(mirrored, own0)
        cols_own1 = taken(native, own1)
        cols_other0 = taken(edges, other0)
        cols_other1 = taken(native, other1)

        parts = [jnp.concatenate([other0, other1], 1)] + rest
        ordered = []
        for h in range(Q):
            chosen = parts[0]
            for j in range(1, Q):
                chosen = jnp.where((p + j) % Q == h, parts[j], chosen)
            ordered.append(chosen)
        other_rows = jnp.concatenate(ordered, 1)

        def weigh(rows, by):
            return (by[:, None] * rows.astype(jnp.float32)).astype(jnp.bfloat16)

        own_rows, other_rows = weigh(slab, weights), weigh(other_rows, other_weights)
        result = product(own_rows, other_rows, cols_own0, cols_other0, None, 0, width)
        return product(own_rows, other_rows, cols_own1, cols_other1, result, 1, width)

    return jax.shard_map(
        on_device,
        mesh=mesh,
        in_specs=(P("pair", "row"), P("pair")),
        out_specs=P("row", ("col", "pair")),
        check_vma=False,
    )
```

```python
import jax
import jax.numpy as jnp
from jax import lax
from jax.experimental import pallas as pl
from jax.experimental.pallas import tpu as pltpu
from jax.sharding import PartitionSpec as P

AXES = ("row", "col", "pair")
LANES = 128
VMEM = pl.BlockSpec(memory_space=pltpu.VMEM)
SMEM = pl.BlockSpec(memory_space=pltpu.SMEM)
ANY = pl.BlockSpec(memory_space=pl.ANY)


def params(mib):
    return pltpu.CompilerParams(vmem_limit_bytes=mib * 2**20)


def product(source, rows, own, other, result, first, columns):
    depth, height = rows.shape
    pairs, width = own[0].shape
    tile = 1024 if height % 1024 == 0 else height
    args = [source, rows, *own, *other]
    in_specs = [SMEM] + [VMEM] * (len(args) - 1)
    aliases = {}
    if result is not None:
        aliases = {len(args): 0}
        in_specs.append(ANY)
        args.append(result)

    def kernel(source, rows, *refs):
        out, held = refs[-2:]

        @pl.when(pl.program_id(0) == 0)
        def _():
            for part, choices in ((pl.ds(0, pairs), own), (pl.ds(pairs, depth - pairs), other)):
                skip = 0 if choices is own else len(own)
                for i in range(len(choices)):
                    here = source[0] == i if i < len(choices) - 1 else source[0] >= i

                    @pl.when(here)
                    def _(part=part, i=skip + i):
                        held[part, :] = refs[i][...]

        at = pl.ds(pl.multiple_of(pl.program_id(0) * tile, tile), tile)
        out[...] = lax.dot_general(
            rows[:, at], held[...], (((0,), (0,)), ((), ())), preferred_element_type=jnp.float32
        )

    return pl.pallas_call(
        kernel,
        grid=(height // tile,),
        in_specs=in_specs,
        out_specs=pl.BlockSpec((pl.Element(tile), pl.Element(width)), lambda i: (i * tile, first)),
        out_shape=jax.ShapeDtypeStruct((height, columns), jnp.float32),
        scratch_shapes=[pltpu.VMEM((depth, width), jnp.bfloat16)],
        input_output_aliases=aliases,
        compiler_params=params(24),
        cost_estimate=pl.CostEstimate(
            flops=2 * height * width * depth, bytes_accessed=4 * height * width, transcendentals=0
        ),
    )(*args)


def weigh(index, slab, weights, other_parts, other_weights, width):
    pairs, height = slab.shape
    others = other_weights.shape[0]
    count = len(other_parts)
    step = 64 if pairs % 64 == 0 else pairs

    def kernel(index, slab, weights, other_weights, *refs):
        parts, out = refs[:count], refs[-1]

        def scaled(by, rows):
            return (by * rows.astype(jnp.float32)).astype(out.dtype)

        @pl.loop(0, pairs // step)
        def _(i):
            at = pl.ds(pl.multiple_of(i * step, step), step)
            out[at, :] = scaled(weights[at, :], slab[at, :])

        @pl.loop(0, others // step)
        def _(i):
            at = pl.ds(pl.multiple_of(i * step, step), step)
            to = pl.ds(pl.multiple_of(pairs + i * step, step), step)
            by = other_weights[at, :]
            offset = 0
            for part in parts:
                size = part.shape[1]
                start = lax.rem(index[0] * width + offset, height)
                out[to, pl.ds(pl.multiple_of(start, LANES), size)] = scaled(by, part[at, :])
                offset += size

    return pl.pallas_call(
        kernel,
        in_specs=[SMEM] + [VMEM] * (3 + count),
        out_specs=VMEM,
        out_shape=jax.ShapeDtypeStruct((pairs + others, height), slab.dtype),
        compiler_params=params(16),
    )(index, slab, weights[:, None], other_weights[:, None], *other_parts)


def assemble(core, mine, theirs, start, size, *earlier):
    count = len(mine)
    half = mine[0].shape[0]

    def kernel(core, *refs):
        out = refs[-1]
        for i in range(count):
            for rows, ref in ((core[0], refs[i]), (1 - core[0], refs[count + i])):
                at = pl.multiple_of((2 * i + rows) * half, half)
                out[pl.ds(at, half), :] = ref[:, start : start + size]

    return pl.pallas_call(
        kernel,
        in_specs=[SMEM] + [VMEM] * (2 * count) + [ANY] * len(earlier),
        out_specs=VMEM,
        out_shape=jax.ShapeDtypeStruct((2 * count * half, size), mine[0].dtype),
        compiler_params=params(16),
    )(core, *mine, *theirs, *earlier)


def hold(values, *earlier):
    count = len(values)

    def kernel(*refs):
        for value, out in zip(refs[:count], refs[-count:]):
            out[...] = value[...]

    return pl.pallas_call(
        kernel,
        in_specs=[VMEM] * count + [ANY] * len(earlier),
        out_specs=[VMEM] * count,
        out_shape=[jax.ShapeDtypeStruct(v.shape, v.dtype) for v in values],
        compiler_params=params(16),
    )(*values, *earlier)


def pick_senders(planes, columns, stage):
    per_side = columns // 2
    sends = [(k, b, t, side) for k, (_, part) in enumerate(stage) for b, t, side in part]
    chosen = [b // per_side if side is None else side for _, b, _, side in sends]

    def cost():
        load = {}
        for (k, b, t, _), side in zip(sends, chosen):
            way = 1 if t > b else -1
            links = [(side, z, way) for z in range(b, t, way)]
            if side != b // per_side:
                links.append((t, side, "across"))
            for link in links:
                load[link] = load.get(link, 0) + stage[k][0]
        return sum(value**6 for value in load.values())

    for i in sorted(range(len(sends)), key=lambda i: -abs(sends[i][1] - sends[i][2])):
        k, b, _, free = sends[i]
        if free is None and sum(s[:2] == (k, b) and c == chosen[i] for s, c in zip(sends, chosen)) > per_side:
            chosen[i] = 1 - chosen[i]
    best = cost()
    better = True
    while better:
        better = False
        for i, (k, b, _, free) in enumerate(sends):
            others = [j for j in range(len(sends)) if j > i and sends[j][3] is None]
            for flips in [[i]] + [[i, j] for j in others]:
                if free is not None:
                    continue
                before = list(chosen)
                for j in flips:
                    chosen[j] = 1 - chosen[j]
                full = any(
                    sum(s[:2] == sends[j][:2] and c == chosen[j] for s, c in zip(sends, chosen)) > per_side
                    for j in flips
                )
                value = best if full else cost()
                if value < best:
                    best, better = value, True
                else:
                    chosen[:] = before
    result = [{} for _ in stage]
    for (k, b, t, free), side in zip(sends, chosen):
        used = [c for (x, _), c in result[k].items() if x == b]
        columns_left = [c for c in range(side * per_side, (side + 1) * per_side) if c not in used]
        result[k][b, t] = columns_left[0] if free is None else b
    return result


def solution(mesh):
    R, C, Q = (mesh.shape[axis] for axis in AXES)
    every = [(b, t, None) for b in range(R) for t in range(R) if b != t]
    ends = [(b, t) for b, t, _ in every if t in (0, R - 1) and abs(b - t) > 1]
    forwards = [(1 if t == 0 else R - 2, t, b // (C // 2)) for b, t in ends]
    near, direct_own = pick_senders(R, C, [(3, [s for s in every if s[:2] not in ends]), (5, every)])
    _, direct_first = pick_senders(R, C, [(3, forwards), (5, every)])
    (direct_last,) = pick_senders(R, C, [(1, every)])

    def number(r, c, p):
        return (r * C + c) * Q + p

    def permute(block, moves):
        pairs = [(number(*source), number(*target)) for source, target in moves]
        return lax.ppermute(block, AXES, pairs) if pairs else jnp.zeros_like(block)

    def permute_all(block, route):
        every = [(r, c, p) for r in range(R) for c in range(C) for p in range(Q)]
        return permute(block, [(device, route(*device)) for device in every])

    def send(block, senders):
        return permute(
            block, [((b, c, p), (t, b, p)) for (b, t), c in senders.items() for p in range(Q)]
        )

    def forward(block):
        moves = [((1, b), (0, b)) for b in range(2, C)]
        moves += [((R - 2, b), (R - 1, b)) for b in range(R - 2)]
        return permute(block, [((*s, p), (*t, p)) for s, t in moves for p in range(Q)])

    def on_device(slab, weights):
        pairs, block = slab.shape
        width = block // Q
        wide = max(LANES, width * 5 // 8 // LANES * LANES)
        shifts = range(1, Q)
        r, c, p = (lax.axis_index(axis) for axis in AXES)
        core = c % 2

        def scalar(value):
            return value.astype(jnp.int32).reshape(1)

        far = ((r == 0) & (c >= 2)) | ((r == R - 1) & (c <= R - 3))
        source = scalar(jnp.where(r == c, 0, jnp.where(far, 2, 1)))
        core_index = scalar(core)

        def own_columns(start, size):
            return lax.dynamic_slice_in_dim(slab, p * width + start, size, 1)

        def share(shift, relative):
            start = (p - shift + relative) % Q * width
            return lax.dynamic_slice(slab, (core * (pairs // 2), start), (pairs // 2, width))

        def exchange(shares):
            return [
                permute_all(m, lambda r, c, p: (r, c, (p - s) % Q)) for s, m in zip(shifts, shares)
            ]

        def swap(mine):
            return [permute_all(m, lambda r, c, p: (r, c ^ 1, p)) for m in mine]

        own0, own1 = own_columns(0, wide), own_columns(wide, width - wide)
        near1, direct0 = send(own1, near), send(own0, direct_own)
        mine = hold(exchange([share(s, 0) for s in shifts]), near1)
        theirs = swap(mine)
        rest_mine = [exchange(hold([share(s, j) for s in shifts], *mine)) for j in range(1, Q)]
        far1 = forward(near1)
        other0 = assemble(core_index, mine, theirs, 0, wide, direct0)
        other1 = assemble(core_index, mine, theirs, wide, width - wide)
        direct_other0 = send(other0, direct_first)
        rest = [assemble(core_index, m, swap(m), 0, width) for m in rest_mine]
        other_weights = jnp.concatenate(
            [permute_all(weights, lambda r, c, p: (r, c, (p - s) % Q)) for s in shifts]
        )
        rows = weigh(scalar(p), slab, weights, [other0, other1, *rest], other_weights, width)
        direct_other1 = send(hold([other1], rows, far1, direct_other0)[0], direct_last)
        result = product(source, rows, [own0, direct0], [other0, direct_other0], None, 0, width)
        return product(
            source, rows, [own1, near1, far1], [other1, direct_other1], result, wide, width
        )

    return jax.shard_map(
        on_device,
        mesh=mesh,
        in_specs=(P("pair", "row"), P("pair")),
        out_specs=P("row", ("col", "pair")),
        check_vma=False,
    )
```

```python
import jax
import jax.numpy as jnp
from jax import lax
from jax.experimental import pallas as pl
from jax.experimental.pallas import tpu as pltpu
from jax.sharding import PartitionSpec as P

AXES = ("row", "col", "pair")
LANES = 128
VMEM = pl.BlockSpec(memory_space=pltpu.VMEM)
SMEM = pl.BlockSpec(memory_space=pltpu.SMEM)
ANY = pl.BlockSpec(memory_space=pl.ANY)


def params(mib):
    return pltpu.CompilerParams(vmem_limit_bytes=mib * 2**20)


def product(source, rows, own, other, result, first, columns):
    depth, height = rows.shape
    pairs, width = own[0].shape
    tile = 1024 if height % 1024 == 0 else height
    args = [source, rows, *own, *other]
    in_specs = [SMEM] + [VMEM] * (len(args) - 1)
    aliases = {}
    if result is not None:
        aliases = {len(args): 0}
        in_specs.append(ANY)
        args.append(result)

    def kernel(source, rows, *refs):
        out, held = refs[-2:]

        @pl.when(pl.program_id(0) == 0)
        def _():
            for part, choices in ((pl.ds(0, pairs), own), (pl.ds(pairs, depth - pairs), other)):
                skip = 0 if choices is own else len(own)
                for i in range(len(choices)):
                    here = source[0] == i if i < len(choices) - 1 else source[0] >= i

                    @pl.when(here)
                    def _(part=part, i=skip + i):
                        held[part, :] = refs[i][...]

        at = pl.ds(pl.multiple_of(pl.program_id(0) * tile, tile), tile)
        out[...] = lax.dot_general(
            rows[:, at], held[...], (((0,), (0,)), ((), ())), preferred_element_type=jnp.float32
        )

    return pl.pallas_call(
        kernel,
        grid=(height // tile,),
        in_specs=in_specs,
        out_specs=pl.BlockSpec((pl.Element(tile), pl.Element(width)), lambda i: (i * tile, first)),
        out_shape=jax.ShapeDtypeStruct((height, columns), jnp.float32),
        scratch_shapes=[pltpu.VMEM((depth, width), jnp.bfloat16)],
        input_output_aliases=aliases,
        compiler_params=params(24),
        cost_estimate=pl.CostEstimate(
            flops=2 * height * width * depth, bytes_accessed=4 * height * width, transcendentals=0
        ),
    )(*args)


def weigh(index, slab, weights, other_parts, other_weights, width):
    pairs, height = slab.shape
    others = other_weights.shape[0]
    count = len(other_parts)
    step = 64 if pairs % 64 == 0 else pairs

    def kernel(index, slab, weights, other_weights, *refs):
        parts, out = refs[:count], refs[-1]

        def scaled(by, rows):
            return (by * rows.astype(jnp.float32)).astype(out.dtype)

        @pl.loop(0, pairs // step)
        def _(i):
            at = pl.ds(pl.multiple_of(i * step, step), step)
            out[at, :] = scaled(weights[at, :], slab[at, :])

        @pl.loop(0, others // step)
        def _(i):
            at = pl.ds(pl.multiple_of(i * step, step), step)
            to = pl.ds(pl.multiple_of(pairs + i * step, step), step)
            by = other_weights[at, :]
            offset = 0
            for part in parts:
                size = part.shape[1]
                start = lax.rem(index[0] * width + offset, height)
                out[to, pl.ds(pl.multiple_of(start, LANES), size)] = scaled(by, part[at, :])
                offset += size

    return pl.pallas_call(
        kernel,
        in_specs=[SMEM] + [VMEM] * (3 + count),
        out_specs=VMEM,
        out_shape=jax.ShapeDtypeStruct((pairs + others, height), slab.dtype),
        compiler_params=params(16),
    )(index, slab, weights[:, None], other_weights[:, None], *other_parts)


def cut_out(starts, slab, shapes):
    count = len(shapes)

    def kernel(starts, slab, *refs):
        outs, done = refs[:count], refs[-1]
        copies = []
        for i, (rows, size) in enumerate(shapes):
            at = pl.ds(pl.multiple_of(starts[2 * i], 16), rows)
            across = pl.ds(pl.multiple_of(starts[2 * i + 1], LANES), size)
            copies.append(pltpu.make_async_copy(slab.at[at, across], outs[i], done.at[i]))
        for copy in copies:
            copy.start()
        for copy in copies:
            copy.wait()

    return pl.pallas_call(
        kernel,
        in_specs=[SMEM, ANY],
        out_specs=[VMEM] * count,
        out_shape=[jax.ShapeDtypeStruct(shape, slab.dtype) for shape in shapes],
        scratch_shapes=[pltpu.SemaphoreType.DMA((count,))],
        compiler_params=params(16),
    )(starts, slab)


def assemble(core, pieces, *earlier):
    count = len(pieces[0][0])
    half = pieces[0][0][0].shape[0]
    sizes = [mine[0].shape[1] for mine, _ in pieces]

    def kernel(core, *refs):
        out = refs[-1]
        refs = list(refs)
        start = 0
        for size in sizes:
            for first in (core[0], 1 - core[0]):
                for i in range(count):
                    at = pl.multiple_of((2 * i + first) * half, half)
                    out[pl.ds(at, half), start : start + size] = refs.pop(0)[...]
            start += size

    parts = [array for mine, theirs in pieces for array in (*mine, *theirs)]
    return pl.pallas_call(
        kernel,
        in_specs=[SMEM] + [VMEM] * len(parts) + [ANY] * len(earlier),
        out_specs=VMEM,
        out_shape=jax.ShapeDtypeStruct((2 * count * half, sum(sizes)), parts[0].dtype),
        compiler_params=params(16),
    )(core, *parts, *earlier)


def hold(values, *earlier):
    count = len(values)

    def kernel(*refs):
        for value, out in zip(refs[:count], refs[-count:]):
            out[...] = value[...]

    return pl.pallas_call(
        kernel,
        in_specs=[VMEM] * count + [ANY] * len(earlier),
        out_specs=[VMEM] * count,
        out_shape=[jax.ShapeDtypeStruct(v.shape, v.dtype) for v in values],
        compiler_params=params(16),
    )(*values, *earlier)


def pick_senders(planes, columns, stage):
    per_side = columns // 2
    sends = [(k, b, t, side) for k, (_, part) in enumerate(stage) for b, t, side in part]
    chosen = [b // per_side if side is None else side for _, b, _, side in sends]

    def cost():
        load = {}
        for (k, b, t, _), side in zip(sends, chosen):
            way = 1 if t > b else -1
            links = [(side, z, way) for z in range(b, t, way)]
            if side != b // per_side:
                links.append((t, side, "across"))
            for link in links:
                load[link] = load.get(link, 0) + stage[k][0]
        return sum(value**6 for value in load.values())

    for i in sorted(range(len(sends)), key=lambda i: -abs(sends[i][1] - sends[i][2])):
        k, b, _, free = sends[i]
        if free is None and sum(s[:2] == (k, b) and c == chosen[i] for s, c in zip(sends, chosen)) > per_side:
            chosen[i] = 1 - chosen[i]
    best = cost()
    better = True
    while better:
        better = False
        for i, (k, b, _, free) in enumerate(sends):
            others = [j for j in range(len(sends)) if j > i and sends[j][3] is None]
            for flips in [[i]] + [[i, j] for j in others]:
                if free is not None:
                    continue
                before = list(chosen)
                for j in flips:
                    chosen[j] = 1 - chosen[j]
                full = any(
                    sum(s[:2] == sends[j][:2] and c == chosen[j] for s, c in zip(sends, chosen)) > per_side
                    for j in flips
                )
                value = best if full else cost()
                if value < best:
                    best, better = value, True
                else:
                    chosen[:] = before
    result = [{} for _ in stage]
    for (k, b, t, free), side in zip(sends, chosen):
        used = [c for (x, _), c in result[k].items() if x == b]
        columns_left = [c for c in range(side * per_side, (side + 1) * per_side) if c not in used]
        result[k][b, t] = columns_left[0] if free is None else b
    return result


def solution(mesh):
    R, C, Q = (mesh.shape[axis] for axis in AXES)
    every = [(b, t, None) for b in range(R) for t in range(R) if b != t]
    ends = [(b, t) for b, t, _ in every if t in (0, R - 1) and abs(b - t) > 1]
    forwards = [(1 if t == 0 else R - 2, t, b // (C // 2)) for b, t in ends]
    near, direct_own = pick_senders(R, C, [(3, [s for s in every if s[:2] not in ends]), (5, every)])
    _, direct_first = pick_senders(R, C, [(3, forwards), (5, every)])


    def number(r, c, p):
        return (r * C + c) * Q + p

    def permute(block, moves):
        pairs = [(number(*source), number(*target)) for source, target in moves]
        return lax.ppermute(block, AXES, pairs) if pairs else jnp.zeros_like(block)

    def permute_all(block, route):
        every = [(r, c, p) for r in range(R) for c in range(C) for p in range(Q)]
        return permute(block, [(device, route(*device)) for device in every])

    def send(block, senders):
        return permute(
            block, [((b, c, p), (t, b, p)) for (b, t), c in senders.items() for p in range(Q)]
        )

    def forward(block):
        moves = [((1, b), (0, b)) for b in range(2, C)]
        moves += [((R - 2, b), (R - 1, b)) for b in range(R - 2)]
        return permute(block, [((*s, p), (*t, p)) for s, t in moves for p in range(Q)])

    def on_device(slab, weights):
        pairs, block = slab.shape
        width = block // Q
        wide = max(LANES, width * 5 // 8 // LANES * LANES)
        cut = max(LANES, wide // 2 // LANES * LANES)
        shifts = range(1, Q)
        r, c, p = (lax.axis_index(axis) for axis in AXES)
        core = c % 2

        def scalar(value):
            return value.astype(jnp.int32).reshape(1)

        far = ((r == 0) & (c >= 2)) | ((r == R - 1) & (c <= R - 3))
        source = scalar(jnp.where(r == c, 0, jnp.where(far, 2, 1)))
        core_index = scalar(core)

        def share(shift, relative, offset, size):
            start = (p - shift + relative) % Q * width + offset
            return (core * (pairs // 2), start), (pairs // 2, size)

        def exchange(shares):
            return [
                permute_all(m, lambda r, c, p: (r, c, (p - s) % Q)) for s, m in zip(shifts, shares)
            ]

        def swap(mine):
            return [permute_all(m, lambda r, c, p: (r, c ^ 1, p)) for m in mine]

        spans = [(0, cut), (cut, wide - cut), (wide, width - wide)]
        spans = [(start, size) for start, size in spans if size]
        blocks = [((0, p * width + wide), (pairs, width - wide)), ((0, p * width), (pairs, wide))]
        blocks += [share(s, 0, *span) for span in spans for s in shifts]
        blocks += [share(s, j, 0, width) for j in range(1, Q) for s in shifts]
        starts = jnp.stack([jnp.asarray(x, jnp.int32) for start, _ in blocks for x in start])
        own1, own0, *shares = cut_out(starts, slab, [shape for _, shape in blocks])

        def take():
            return [shares.pop(0) for _ in shifts]

        near1, direct0 = send(own1, near), send(own0, direct_own)
        pieces = []
        for _ in spans:
            m = exchange(take())
            pieces.append((m, swap(m)))
        mine = [m for piece, _ in pieces for m in piece]
        rest_mine = [exchange(hold(take(), *mine)) for j in range(1, Q)]
        far1 = forward(near1)
        other0 = assemble(core_index, pieces[:-1], direct0)
        other1 = assemble(core_index, pieces[-1:])
        direct_other0 = send(other0, direct_first)
        rest_mine = [hold(m, far1) for m in rest_mine]
        rest = [assemble(core_index, [(m, swap(m))]) for m in rest_mine]
        other_weights = jnp.concatenate(
            [permute_all(weights, lambda r, c, p: (r, c, (p - s) % Q)) for s in shifts]
        )
        rows = weigh(scalar(p), slab, weights, [other0, other1, *rest], other_weights, width)
        direct_other1 = send(hold([other1], rows, direct_other0)[0], direct_first)
        result = product(source, rows, [own0, direct0], [other0, direct_other0], None, 0, width)
        return product(
            source, rows, [own1, near1, far1], [other1, direct_other1], result, wide, width
        )

    return jax.shard_map(
        on_device,
        mesh=mesh,
        in_specs=(P("pair", "row"), P("pair")),
        out_specs=P("row", ("col", "pair")),
        check_vma=False,
    )
```

```python
import jax
import jax.numpy as jnp
from jax import lax
from jax.experimental import pallas as pl
from jax.experimental.pallas import tpu as pltpu
from jax.sharding import PartitionSpec as P

AXES = ("row", "col", "pair")
LANES = 128
VMEM = pl.BlockSpec(memory_space=pltpu.VMEM)
SMEM = pl.BlockSpec(memory_space=pltpu.SMEM)
ANY = pl.BlockSpec(memory_space=pl.ANY)


def params(mib):
    return pltpu.CompilerParams(vmem_limit_bytes=mib * 2**20)


def product(source, rows, own, other, result, first, columns):
    depth, height = rows.shape
    pairs, width = own[0].shape[0], other[0].shape[1]
    tile = 1024 if height % 1024 == 0 else height
    args = [source, rows, *own, *other]
    in_specs = [SMEM] + [VMEM] * (len(args) - 1)
    aliases = {}
    if result is not None:
        aliases = {len(args): 0}
        in_specs.append(ANY)
        args.append(result)

    def kernel(source, rows, *refs):
        out, held = refs[-2:]

        @pl.when(pl.program_id(0) == 0)
        def _():
            for part, choices in ((pl.ds(0, pairs), own), (pl.ds(pairs, depth - pairs), other)):
                skip = 0 if choices is own else len(own)
                for i in range(len(choices)):
                    start = first if choices is own else 0

                    @pl.when(source[0] == i)
                    def _(part=part, i=skip + i, start=start):
                        held[part, :] = refs[i][:, start : start + width]

        at = pl.ds(pl.multiple_of(pl.program_id(0) * tile, tile), tile)
        out[...] = lax.dot_general(
            rows[:, at], held[...], (((0,), (0,)), ((), ())), preferred_element_type=jnp.float32
        )

    return pl.pallas_call(
        kernel,
        grid=(height // tile,),
        in_specs=in_specs,
        out_specs=pl.BlockSpec((pl.Element(tile), pl.Element(width)), lambda i: (i * tile, first)),
        out_shape=jax.ShapeDtypeStruct((height, columns), jnp.float32),
        scratch_shapes=[pltpu.VMEM((depth, width), jnp.bfloat16)],
        input_output_aliases=aliases,
        compiler_params=params(24),
        cost_estimate=pl.CostEstimate(
            flops=2 * height * width * depth, bytes_accessed=4 * height * width, transcendentals=0
        ),
    )(*args)


def weigh(index, slab, weights, other_parts, other_weights, width):
    pairs, height = slab.shape
    others = other_weights.shape[0]
    count = len(other_parts)
    step = 64 if pairs % 64 == 0 else pairs

    def kernel(index, slab, weights, other_weights, *refs):
        parts, out = refs[:count], refs[-1]

        def scaled(by, rows):
            return (by * rows.astype(jnp.float32)).astype(out.dtype)

        @pl.loop(0, pairs // step)
        def _(i):
            at = pl.ds(pl.multiple_of(i * step, step), step)
            out[at, :] = scaled(weights[at, :], slab[at, :])

        @pl.loop(0, others // step)
        def _(i):
            at = pl.ds(pl.multiple_of(i * step, step), step)
            to = pl.ds(pl.multiple_of(pairs + i * step, step), step)
            by = other_weights[at, :]
            offset = 0
            for part in parts:
                size = part.shape[1]
                start = lax.rem(index[0] * width + offset, height)
                out[to, pl.ds(pl.multiple_of(start, LANES), size)] = scaled(by, part[at, :])
                offset += size

    return pl.pallas_call(
        kernel,
        in_specs=[SMEM] + [VMEM] * (3 + count),
        out_specs=VMEM,
        out_shape=jax.ShapeDtypeStruct((pairs + others, height), slab.dtype),
        compiler_params=params(16),
    )(index, slab, weights[:, None], other_weights[:, None], *other_parts)


def cut_out(starts, slab, shapes):
    count = len(shapes)

    def kernel(starts, slab, *refs):
        outs, done = refs[:count], refs[-1]
        copies = []
        for i, (rows, size) in enumerate(shapes):
            at = pl.ds(pl.multiple_of(starts[2 * i], 16), rows)
            across = pl.ds(pl.multiple_of(starts[2 * i + 1], LANES), size)
            copies.append(pltpu.make_async_copy(slab.at[at, across], outs[i], done.at[i]))
        for copy in copies:
            copy.start()
        for copy in copies:
            copy.wait()

    return pl.pallas_call(
        kernel,
        in_specs=[SMEM, ANY],
        out_specs=[VMEM] * count,
        out_shape=[jax.ShapeDtypeStruct(shape, slab.dtype) for shape in shapes],
        scratch_shapes=[pltpu.SemaphoreType.DMA((count,))],
        compiler_params=params(16),
    )(starts, slab)


def assemble(core, mine, theirs, start, size):
    count = len(mine)
    half = mine[0].shape[0]

    def kernel(core, *refs):
        out = refs[-1]
        for i in range(count):
            for rows, ref in ((core[0], refs[i]), (1 - core[0], refs[count + i])):
                at = pl.multiple_of((2 * i + rows) * half, half)
                out[pl.ds(at, half), :] = ref[:, start : start + size]

    return pl.pallas_call(
        kernel,
        in_specs=[SMEM] + [VMEM] * (2 * count),
        out_specs=VMEM,
        out_shape=jax.ShapeDtypeStruct((2 * count * half, size), mine[0].dtype),
        compiler_params=params(16),
    )(core, *mine, *theirs)


def hold(values, *earlier):
    count = len(values)

    def kernel(*refs):
        for value, out in zip(refs[:count], refs[-count:]):
            out[...] = value[...]

    return pl.pallas_call(
        kernel,
        in_specs=[VMEM] * count + [ANY] * len(earlier),
        out_specs=[VMEM] * count,
        out_shape=[jax.ShapeDtypeStruct(v.shape, v.dtype) for v in values],
        compiler_params=params(16),
    )(*values, *earlier)


def pick_senders(planes, columns):
    per_side = columns // 2
    sends = [(b, t) for b in range(planes) for t in range(planes) if b != t]

    def cost(chosen):
        load, sources = {}, {}
        for (b, t), side in zip(sends, chosen):
            way = 1 if t > b else -1
            links = [(side, z, way) for z in range(b, t, way)]
            if side != b // per_side:
                links.append((t, side, "across"))
            for link in links:
                load[link] = load.get(link, 0) + 1
                sources.setdefault(link, set()).add(b)
        return sum(value**6 * (4 + len(sources[link])) for link, value in load.items())

    def full(chosen, i):
        return sum(s[0] == sends[i][0] and c == chosen[i] for s, c in zip(sends, chosen)) > per_side

    def settle(chosen):
        for i in sorted(range(len(sends)), key=lambda i: -abs(sends[i][0] - sends[i][1])):
            if full(chosen, i):
                chosen[i] = 1 - chosen[i]
        every = range(len(sends))
        best, better = cost(chosen), True
        while better:
            better = False
            for flips in [[i] for i in every] + [[i, j] for i in every for j in range(i)]:
                trial = list(chosen)
                for j in flips:
                    trial[j] = 1 - trial[j]
                if not any(full(trial, j) for j in flips) and cost(trial) < best:
                    chosen, best, better = trial, cost(trial), True
        return best, chosen

    def native(b, t):
        return b // per_side

    def apart(b, t):
        inward = t < b if b >= planes // 2 else t > b
        return 1 - native(b, t) if inward and (b not in (0, planes - 1) or abs(b - t) == 1) else native(b, t)

    starts = [[rule(*send) for send in sends] for rule in (native, apart)]
    _, chosen = min((settle(start) for start in starts), key=lambda result: result[0])
    result = {}
    for (b, t), side in zip(sends, chosen):
        used = [c for (x, _), c in result.items() if x == b]
        result[b, t] = [c for c in range(side * per_side, (side + 1) * per_side) if c not in used][0]
    return result


def solution(mesh):
    R, C, Q = (mesh.shape[axis] for axis in AXES)
    senders = pick_senders(R, C)

    def number(r, c, p):
        return (r * C + c) * Q + p

    def permute(block, moves):
        pairs = [(number(*source), number(*target)) for source, target in moves]
        return lax.ppermute(block, AXES, pairs) if pairs else jnp.zeros_like(block)

    def permute_all(block, route):
        every = [(r, c, p) for r in range(R) for c in range(C) for p in range(Q)]
        return permute(block, [(device, route(*device)) for device in every])

    def send(block):
        return permute(
            block, [((b, c, p), (t, b, p)) for (b, t), c in senders.items() for p in range(Q)]
        )

    def on_device(slab, weights):
        pairs, block = slab.shape
        width = block // Q
        wide = max(LANES, width * 5 // 8 // LANES * LANES)
        shifts = range(1, Q)
        r, c, p = (lax.axis_index(axis) for axis in AXES)
        core = c % 2

        def scalar(value):
            return value.astype(jnp.int32).reshape(1)

        source = scalar(jnp.where(r == c, 0, 1))
        core_index = scalar(core)

        def share(shift, relative, offset, size):
            start = (p - shift + relative) % Q * width + offset
            return (core * (pairs // 2), start), (pairs // 2, size)

        def exchange(shares):
            return [
                permute_all(m, lambda r, c, p: (r, c, (p - s) % Q)) for s, m in zip(shifts, shares)
            ]

        def swap(mine):
            return [permute_all(m, lambda r, c, p: (r, c ^ 1, p)) for m in mine]

        blocks = [((0, p * width), (pairs, width))]
        blocks += [share(s, j, 0, width) for j in range(Q) for s in shifts]
        starts = jnp.stack([jnp.asarray(x, jnp.int32) for start, _ in blocks for x in start])
        own, *shares = cut_out(starts, slab, [shape for _, shape in blocks])
        shares = [shares[i : i + Q - 1] for i in range(0, len(shares), Q - 1)]

        direct_own = send(own)
        mine = exchange(shares[0])
        theirs = swap(mine)
        others = [
            assemble(core_index, mine, theirs, start, size)
            for start, size in ((0, wide), (wide, width - wide))
        ]
        direct_other0 = send(others[0])
        rest = []
        for part in shares[1:]:
            received = hold(exchange(hold(part, *mine)), direct_own)
            rest.append(assemble(core_index, received, swap(received), 0, width))
        other_weights = jnp.concatenate(
            [permute_all(weights, lambda r, c, p: (r, c, (p - s) % Q)) for s in shifts]
        )
        rows = weigh(scalar(p), slab, weights, [*others, *rest], other_weights, width)
        direct_other1 = send(hold(others[1:], rows)[0])
        columns = [own, direct_own]
        result = product(source, rows, columns, [others[0], direct_other0], None, 0, width)
        return product(source, rows, columns, [others[1], direct_other1], result, wide, width)

    return jax.shard_map(
        on_device,
        mesh=mesh,
        in_specs=(P("pair", "row"), P("pair")),
        out_specs=P("row", ("col", "pair")),
        check_vma=False,
    )
```

```python
import jax
import jax.numpy as jnp
from jax import lax
from jax.experimental import pallas as pl
from jax.experimental.pallas import tpu as pltpu
from jax.sharding import PartitionSpec as P

AXES = ("row", "col", "pair")
LANES = 128
PLACE, CORE, OWN_OR_SENT, STARTS = range(4)
PARTS = 3
VMEM = pl.BlockSpec(memory_space=pltpu.VMEM)
SMEM = pl.BlockSpec(memory_space=pltpu.SMEM)
ANY = pl.BlockSpec(memory_space=pl.ANY)
HBM = pl.BlockSpec(memory_space=pltpu.HBM)


def params(mib):
    return pltpu.CompilerParams(vmem_limit_bytes=mib * 2**20)


def product(places, rows, own, other, result, first, columns):
    depth, height = rows.shape
    pairs, width = own[0].shape[0], other[0].shape[1]
    tile = 1024 if height % 1024 == 0 else height
    args = [places, rows, *own, *other]
    in_specs = [SMEM] + [VMEM] * (len(args) - 1)
    aliases = {}
    if result is not None:
        aliases = {len(args): 0}
        in_specs.append(ANY)
        args.append(result)

    def kernel(places, rows, *refs):
        out, held = refs[-2:]

        @pl.when(pl.program_id(0) == 0)
        def _():
            for part, choices in ((pl.ds(0, pairs), own), (pl.ds(pairs, depth - pairs), other)):
                skip = 0 if choices is own else len(own)
                for i in range(len(choices)):
                    start = first if choices is own else 0

                    @pl.when(places[OWN_OR_SENT] == i)
                    def _(part=part, i=skip + i, start=start):
                        held[part, :] = refs[i][:, start : start + width]

        at = pl.ds(pl.multiple_of(pl.program_id(0) * tile, tile), tile)
        out[...] = lax.dot_general(
            rows[:, at], held[...], (((0,), (0,)), ((), ())), preferred_element_type=jnp.float32
        )

    return pl.pallas_call(
        kernel,
        grid=(height // tile,),
        in_specs=in_specs,
        out_specs=pl.BlockSpec((pl.Element(tile), pl.Element(width)), lambda i: (i * tile, first)),
        out_shape=jax.ShapeDtypeStruct((height, columns), jnp.float32),
        scratch_shapes=[pltpu.VMEM((depth, width), jnp.bfloat16)],
        input_output_aliases=aliases,
        compiler_params=params(5 + (8 * tile + 2 * depth) * width // 2**20),
        cost_estimate=pl.CostEstimate(
            flops=2 * height * width * depth, bytes_accessed=4 * height * width, transcendentals=0
        ),
    )(*args)


def weigh(places, slab, weights, others, rest, other_weights, width):
    pairs, height = slab.shape
    half = pairs // 2
    shifts = len(rest[0][0])
    step = 64 if half % 64 == 0 else half
    arrays = [*others, *(m for mine, theirs in rest for m in (*mine, *theirs))]

    def kernel(places, slab, weights, other_weights, *refs):
        *refs, out, own, arrived = refs
        fetch = pltpu.make_async_copy(slab, own, arrived)
        fetch.start()

        def put(rows, by, ref, at, column):
            start = pl.multiple_of(lax.rem(places[PLACE] * width + column, height), LANES)
            to = pl.ds(pl.multiple_of(pairs + rows, step), step)
            value = by[pl.ds(pl.multiple_of(rows, step), step), :] * ref[at, :].astype(jnp.float32)
            out[to, pl.ds(start, ref.shape[1])] = value.astype(out.dtype)

        @pl.loop(0, shifts * pairs // step)
        def _(i):
            at = pl.ds(pl.multiple_of(i * step, step), step)
            column = 0
            for ref in refs[: len(others)]:
                put(i * step, other_weights, ref, at, column)
                column += ref.shape[1]

        @pl.loop(0, half // step)
        def _(i):
            at = pl.ds(pl.multiple_of(i * step, step), step)
            parts = iter(refs[len(others) :])
            column = width
            for mine, _ in rest:
                for first in (places[CORE], 1 - places[CORE]):
                    for shift in range(shifts):
                        put(shift * pairs + first * half + i * step, other_weights, next(parts), at, column)
                column += mine[0].shape[1]

        fetch.wait()

        @pl.loop(0, pairs // step)
        def _(i):
            at = pl.ds(pl.multiple_of(i * step, step), step)
            out[at, :] = (weights[at, :] * own[at, :].astype(jnp.float32)).astype(out.dtype)

    return pl.pallas_call(
        kernel,
        in_specs=[SMEM, HBM] + [VMEM] * (2 + len(arrays)),
        out_specs=VMEM,
        out_shape=jax.ShapeDtypeStruct(((1 + shifts) * pairs, height), slab.dtype),
        scratch_shapes=[pltpu.VMEM(slab.shape, slab.dtype), pltpu.SemaphoreType.DMA],
        compiler_params=params(3 + 2 * pairs * height // 2**20),
    )(places, slab, weights[:, None], other_weights[:, None], *arrays)


def split(width, count, last):
    lanes = (width - last) // LANES
    count = min(count, lanes)
    sizes = [LANES * (lanes // count + (i < lanes % count)) for i in range(count)] + [last] * (last > 0)
    return [(sum(sizes[:i]), size) for i, size in enumerate(sizes)]


def cut_out(places, slab, shapes):
    count = len(shapes)

    def kernel(places, slab, *refs):
        outs, done = refs[:count], refs[-1]
        copies = []
        for i, (rows, size) in enumerate(shapes):
            at = pl.ds(pl.multiple_of(places[STARTS + 2 * i], 16), rows)
            across = pl.ds(pl.multiple_of(places[STARTS + 2 * i + 1], LANES), size)
            copies.append(pltpu.make_async_copy(slab.at[at, across], outs[i], done.at[i]))
        for copy in copies:
            copy.start()
        for copy in copies:
            copy.wait()

    return pl.pallas_call(
        kernel,
        in_specs=[SMEM, HBM],
        out_specs=[VMEM] * count,
        out_shape=[jax.ShapeDtypeStruct(shape, slab.dtype) for shape in shapes],
        scratch_shapes=[pltpu.SemaphoreType.DMA((count,))],
        compiler_params=params(2),
    )(places, slab)


def assemble(places, mine, theirs, start, size, *earlier):
    count = len(mine)
    half = mine[0].shape[0]

    def kernel(places, *refs):
        out = refs[-1]
        for i in range(count):
            for rows, ref in ((places[CORE], refs[i]), (1 - places[CORE], refs[count + i])):
                at = pl.multiple_of((2 * i + rows) * half, half)
                out[pl.ds(at, half), :] = ref[:, start : start + size]

    return pl.pallas_call(
        kernel,
        in_specs=[SMEM] + [VMEM] * (2 * count) + [ANY] * len(earlier),
        out_specs=VMEM,
        out_shape=jax.ShapeDtypeStruct((2 * count * half, size), mine[0].dtype),
        compiler_params=params(2),
    )(places, *mine, *theirs, *earlier)


def hold(values, spans, *earlier):
    count = len(values)

    def kernel(*refs):
        outs = iter(refs[count + len(earlier) :])
        for start, size in spans:
            for value in refs[:count]:
                next(outs)[...] = value[:, start : start + size]

    outs = pl.pallas_call(
        kernel,
        in_specs=[VMEM] * count + [ANY] * len(earlier),
        out_specs=[VMEM] * (count * len(spans)),
        out_shape=[jax.ShapeDtypeStruct((v.shape[0], n), v.dtype) for _, n in spans for v in values],
        compiler_params=params(2),
    )(*values, *earlier)
    return [outs[i : i + count] for i in range(0, len(outs), count)]


def pick_senders(planes, columns):
    per_side = columns // 2
    sends = [(b, t) for b in range(planes) for t in range(planes) if b != t]

    def cost(chosen):
        load, sources = {}, {}
        for (b, t), side in zip(sends, chosen):
            way = 1 if t > b else -1
            links = [(side, z, way) for z in range(b, t, way)]
            if side != b // per_side:
                links.append((t, side, "across"))
            for link in links:
                load[link] = load.get(link, 0) + 1
                sources.setdefault(link, set()).add(b)
        return sum(value**6 * (4 + len(sources[link])) for link, value in load.items())

    def full(chosen, i):
        return sum(s[0] == sends[i][0] and c == chosen[i] for s, c in zip(sends, chosen)) > per_side

    def settle(chosen):
        for i in sorted(range(len(sends)), key=lambda i: -abs(sends[i][0] - sends[i][1])):
            if full(chosen, i):
                chosen[i] = 1 - chosen[i]
        every = range(len(sends))
        best, better = cost(chosen), True
        while better:
            better = False
            for flips in [[i] for i in every] + [[i, j] for i in every for j in range(i)]:
                trial = list(chosen)
                for j in flips:
                    trial[j] = 1 - trial[j]
                if not any(full(trial, j) for j in flips) and cost(trial) < best:
                    chosen, best, better = trial, cost(trial), True
        return best, chosen

    def native(b, t):
        return b // per_side

    def apart(b, t):
        inward = t < b if b >= planes // 2 else t > b
        return 1 - native(b, t) if inward and (b not in (0, planes - 1) or abs(b - t) == 1) else native(b, t)

    starts = [[rule(*send) for send in sends] for rule in (native, apart)]
    _, chosen = min((settle(start) for start in starts), key=lambda result: result[0])
    result = {}
    for (b, t), side in zip(sends, chosen):
        used = [c for (x, _), c in result.items() if x == b]
        result[b, t] = [c for c in range(side * per_side, (side + 1) * per_side) if c not in used][0]
    return result


def solution(mesh):
    R, C, Q = (mesh.shape[axis] for axis in AXES)
    senders = pick_senders(R, C)

    def number(r, c, p):
        return (r * C + c) * Q + p

    def permute(block, moves):
        pairs = [(number(*source), number(*target)) for source, target in moves]
        return lax.ppermute(block, AXES, pairs) if pairs else jnp.zeros_like(block)

    def permute_all(block, route):
        every = [(r, c, p) for r in range(R) for c in range(C) for p in range(Q)]
        return permute(block, [(device, route(*device)) for device in every])

    def send(block):
        return permute(
            block, [((b, c, p), (t, b, p)) for (b, t), c in senders.items() for p in range(Q)]
        )

    def on_device(slab, weights):
        pairs, block = slab.shape
        width = block // Q
        spans = split(width, PARTS - 1, max(LANES, width * 1 // 4 // LANES * LANES))
        halves = split(width, 2, 0)
        shifts = range(1, Q)
        r, c, p = (lax.axis_index(axis) for axis in AXES)
        core = c % 2

        def share(shift, relative, offset, size):
            start = (p - shift + relative) % Q * width + offset
            return (core * (pairs // 2), start), (pairs // 2, size)

        def exchange(shares):
            return [
                permute_all(m, lambda r, c, p: (r, c, (p - s) % Q)) for s, m in zip(shifts, shares)
            ]

        def swap(mine):
            return [permute_all(m, lambda r, c, p: (r, c ^ 1, p)) for m in mine]

        blocks = [((0, p * width), (pairs, width))]
        blocks += [share(s, j, 0, width) for j in range(Q) for s in shifts]
        starts = [x for start, _ in blocks for x in start]
        places = jnp.stack([jnp.asarray(x, jnp.int32) for x in (p, core, jnp.where(r == c, 0, 1), *starts)])
        own, *shares = cut_out(places, slab, [shape for _, shape in blocks])
        shares = [shares[i : i + Q - 1] for i in range(0, len(shares), Q - 1)]

        other_weights = jnp.concatenate(
            [permute_all(weights, lambda r, c, p: (r, c, (p - s) % Q)) for s in shifts]
        )
        direct_own = send(own)
        mine = exchange(shares[0])
        theirs = swap(mine)
        others = [assemble(places, mine, theirs, *span) for span in spans]
        direct_others = [send(others[0])]
        rest = []
        for part in shares[1:]:
            part = hold(part, [(0, width)], other_weights)[0]
            for piece in hold(part, halves, *mine):
                received = exchange(piece)
                received = hold(received, [(0, received[0].shape[1])], direct_own)[0]
                rest.append((received, swap(received)))
        rows = weigh(places, slab, weights, others, rest, other_weights, width)
        for i, other in enumerate(others[1:], 1):
            earlier = rows if i == len(others) - 1 else direct_own
            direct_others.append(send(hold([other], [(0, other.shape[1])], earlier)[0][0]))
        result = None
        for other, sent, (start, _) in zip(others, direct_others, spans):
            result = product(places, rows, [own, direct_own], [other, sent], result, start, width)
        return result

    return jax.shard_map(
        on_device,
        mesh=mesh,
        in_specs=(P("pair", "row"), P("pair")),
        out_specs=P("row", ("col", "pair")),
        check_vma=False,
    )
```

```python
import jax
import jax.numpy as jnp
from jax import lax
from jax.experimental import pallas as pl
from jax.experimental.pallas import tpu as pltpu
from jax.sharding import PartitionSpec as P

AXES = ("row", "col", "pair")
LANES = 128
PLACE, CORE, OWN_OR_SENT, STARTS = range(4)
PARTS = 3
VMEM = pl.BlockSpec(memory_space=pltpu.VMEM)
SMEM = pl.BlockSpec(memory_space=pltpu.SMEM)
ANY = pl.BlockSpec(memory_space=pl.ANY)
HBM = pl.BlockSpec(memory_space=pltpu.HBM)


def params(mib):
    return pltpu.CompilerParams(vmem_limit_bytes=mib * 2**20)


def product(places, rows, own, other, result, first, columns):
    depth, height = rows.shape
    pairs, width = own[0].shape[0], other[0].shape[1]
    tile = 1024 if height % 1024 == 0 else height
    args = [places, rows, *own, *other]
    in_specs = [SMEM] + [VMEM] * (len(args) - 1)
    aliases = {}
    if result is not None:
        aliases = {len(args): 0}
        in_specs.append(ANY)
        args.append(result)

    def kernel(places, rows, *refs):
        out, held = refs[-2:]

        @pl.when(pl.program_id(0) == 0)
        def _():
            for part, choices in ((pl.ds(0, pairs), own), (pl.ds(pairs, depth - pairs), other)):
                skip = 0 if choices is own else len(own)
                for i in range(len(choices)):
                    start = first if choices is own else 0

                    @pl.when(places[OWN_OR_SENT] == i)
                    def _(part=part, i=skip + i, start=start):
                        held[part, :] = refs[i][:, start : start + width]

        at = pl.ds(pl.multiple_of(pl.program_id(0) * tile, tile), tile)
        out[...] = lax.dot_general(
            rows[:, at], held[...], (((0,), (0,)), ((), ())), preferred_element_type=jnp.float32
        )

    return pl.pallas_call(
        kernel,
        grid=(height // tile,),
        in_specs=in_specs,
        out_specs=pl.BlockSpec((pl.Element(tile), pl.Element(width)), lambda i: (i * tile, first)),
        out_shape=jax.ShapeDtypeStruct((height, columns), jnp.float32),
        scratch_shapes=[pltpu.VMEM((depth, width), jnp.bfloat16)],
        input_output_aliases=aliases,
        compiler_params=params(5 + (8 * tile + 2 * depth) * width // 2**20),
        cost_estimate=pl.CostEstimate(
            flops=2 * height * width * depth, bytes_accessed=4 * height * width, transcendentals=0
        ),
    )(*args)


def weigh(places, slab, weights, others, rest, other_weights, width):
    pairs, height = slab.shape
    half = pairs // 2
    shifts = len(rest[0][0])
    step = 64 if half % 64 == 0 else half
    arrays = [*others, *(m for mine, theirs in rest for m in (*mine, *theirs))]

    def kernel(places, slab, weights, other_weights, *refs):
        *refs, out, own, arrived = refs
        fetch = pltpu.make_async_copy(slab, own, arrived)
        fetch.start()

        def put(rows, by, ref, at, column):
            start = pl.multiple_of(lax.rem(places[PLACE] * width + column, height), LANES)
            to = pl.ds(pl.multiple_of(pairs + rows, step), step)
            value = by[pl.ds(pl.multiple_of(rows, step), step), :] * ref[at, :].astype(jnp.float32)
            out[to, pl.ds(start, ref.shape[1])] = value.astype(out.dtype)

        @pl.loop(0, shifts * pairs // step)
        def _(i):
            at = pl.ds(pl.multiple_of(i * step, step), step)
            column = 0
            for ref in refs[: len(others)]:
                put(i * step, other_weights, ref, at, column)
                column += ref.shape[1]

        @pl.loop(0, half // step)
        def _(i):
            at = pl.ds(pl.multiple_of(i * step, step), step)
            parts = iter(refs[len(others) :])
            column = width
            for mine, _ in rest:
                for first in (places[CORE], 1 - places[CORE]):
                    for shift in range(shifts):
                        put(shift * pairs + first * half + i * step, other_weights, next(parts), at, column)
                column += mine[0].shape[1]

        fetch.wait()

        @pl.loop(0, pairs // step)
        def _(i):
            at = pl.ds(pl.multiple_of(i * step, step), step)
            out[at, :] = (weights[at, :] * own[at, :].astype(jnp.float32)).astype(out.dtype)

    return pl.pallas_call(
        kernel,
        in_specs=[SMEM, HBM] + [VMEM] * (2 + len(arrays)),
        out_specs=VMEM,
        out_shape=jax.ShapeDtypeStruct(((1 + shifts) * pairs, height), slab.dtype),
        scratch_shapes=[pltpu.VMEM(slab.shape, slab.dtype), pltpu.SemaphoreType.DMA],
        compiler_params=params(3 + 2 * pairs * height // 2**20),
    )(places, slab, weights[:, None], other_weights[:, None], *arrays)


def split(width, count, last):
    lanes = (width - last) // LANES
    count = min(count, lanes)
    sizes = [LANES * (lanes // count + (i < lanes % count)) for i in range(count)] + [last] * (last > 0)
    return [(sum(sizes[:i]), size) for i, size in enumerate(sizes)]


def cut_out(places, slab, shapes):
    count = len(shapes)

    def kernel(places, slab, *refs):
        outs, done = refs[:count], refs[-1]
        copies = []
        for i, (rows, size) in enumerate(shapes):
            at = pl.ds(pl.multiple_of(places[STARTS + 2 * i], 16), rows)
            across = pl.ds(pl.multiple_of(places[STARTS + 2 * i + 1], LANES), size)
            copies.append(pltpu.make_async_copy(slab.at[at, across], outs[i], done.at[i]))
        for copy in copies:
            copy.start()
        for copy in copies:
            copy.wait()

    return pl.pallas_call(
        kernel,
        in_specs=[SMEM, HBM],
        out_specs=[VMEM] * count,
        out_shape=[jax.ShapeDtypeStruct(shape, slab.dtype) for shape in shapes],
        scratch_shapes=[pltpu.SemaphoreType.DMA((count,))],
        compiler_params=params(2),
    )(places, slab)


def assemble(places, pieces, start, size):
    count = len(pieces[0][1])
    half = pieces[0][1][0].shape[0]
    arrays = [array for _, mine, theirs in pieces for array in (*mine, *theirs)]

    def kernel(places, *refs):
        *refs, out = refs
        refs = iter(refs)
        for offset, mine, _ in pieces:
            low, high = max(start, offset), min(start + size, offset + mine[0].shape[1])
            for rows in (places[CORE], 1 - places[CORE]):
                for i in range(count):
                    ref = next(refs)
                    if low < high:
                        at = pl.ds(pl.multiple_of((2 * i + rows) * half, half), half)
                        out[at, low - start : high - start] = ref[:, low - offset : high - offset]

    return pl.pallas_call(
        kernel,
        in_specs=[SMEM] + [VMEM] * len(arrays),
        out_specs=VMEM,
        out_shape=jax.ShapeDtypeStruct((2 * count * half, size), arrays[0].dtype),
        compiler_params=params(2),
    )(places, *arrays)


def hold(values, spans, *earlier):
    count = len(values)

    def kernel(*refs):
        outs = iter(refs[count + len(earlier) :])
        for start, size in spans:
            for value in refs[:count]:
                next(outs)[...] = value[:, start : start + size]

    outs = pl.pallas_call(
        kernel,
        in_specs=[VMEM] * count + [ANY] * len(earlier),
        out_specs=[VMEM] * (count * len(spans)),
        out_shape=[jax.ShapeDtypeStruct((v.shape[0], n), v.dtype) for _, n in spans for v in values],
        compiler_params=params(2),
    )(*values, *earlier)
    return [outs[i : i + count] for i in range(0, len(outs), count)]


def pick_senders(planes, columns):
    per_side = columns // 2
    sends = [(b, t) for b in range(planes) for t in range(planes) if b != t]

    def cost(chosen):
        load, sources = {}, {}
        for (b, t), side in zip(sends, chosen):
            way = 1 if t > b else -1
            links = [(side, z, way) for z in range(b, t, way)]
            if side != b // per_side:
                links.append((t, side, "across"))
            for link in links:
                load[link] = load.get(link, 0) + 1
                sources.setdefault(link, set()).add(b)
        return sum(value**6 * (4 + len(sources[link])) for link, value in load.items())

    def full(chosen, i):
        return sum(s[0] == sends[i][0] and c == chosen[i] for s, c in zip(sends, chosen)) > per_side

    def settle(chosen):
        for i in sorted(range(len(sends)), key=lambda i: -abs(sends[i][0] - sends[i][1])):
            if full(chosen, i):
                chosen[i] = 1 - chosen[i]
        every = range(len(sends))
        best, better = cost(chosen), True
        while better:
            better = False
            for flips in [[i] for i in every] + [[i, j] for i in every for j in range(i)]:
                trial = list(chosen)
                for j in flips:
                    trial[j] = 1 - trial[j]
                if not any(full(trial, j) for j in flips) and cost(trial) < best:
                    chosen, best, better = trial, cost(trial), True
        return best, chosen

    def native(b, t):
        return b // per_side

    def apart(b, t):
        inward = t < b if b >= planes // 2 else t > b
        return 1 - native(b, t) if inward and (b not in (0, planes - 1) or abs(b - t) == 1) else native(b, t)

    starts = [[rule(*send) for send in sends] for rule in (native, apart)]
    _, chosen = min((settle(start) for start in starts), key=lambda result: result[0])
    result = {}
    for (b, t), side in zip(sends, chosen):
        used = [c for (x, _), c in result.items() if x == b]
        result[b, t] = [c for c in range(side * per_side, (side + 1) * per_side) if c not in used][0]
    return result


def solution(mesh):
    R, C, Q = (mesh.shape[axis] for axis in AXES)
    senders = pick_senders(R, C)

    def number(r, c, p):
        return (r * C + c) * Q + p

    def permute(block, moves):
        pairs = [(number(*source), number(*target)) for source, target in moves]
        return lax.ppermute(block, AXES, pairs) if pairs else jnp.zeros_like(block)

    def permute_all(block, route):
        every = [(r, c, p) for r in range(R) for c in range(C) for p in range(Q)]
        return permute(block, [(device, route(*device)) for device in every])

    def send(block):
        return permute(
            block, [((b, c, p), (t, b, p)) for (b, t), c in senders.items() for p in range(Q)]
        )

    def on_device(slab, weights):
        pairs, block = slab.shape
        width = block // Q
        spans = split(width, PARTS - 1, max(LANES, width * 1 // 4 // LANES * LANES))
        halves = split(width, 2, 0)
        shifts = range(1, Q)
        r, c, p = (lax.axis_index(axis) for axis in AXES)
        core = c % 2

        def share(shift, relative, offset, size):
            start = (p - shift + relative) % Q * width + offset
            return (core * (pairs // 2), start), (pairs // 2, size)

        def exchange(shares):
            return [
                permute_all(m, lambda r, c, p: (r, c, (p - s) % Q)) for s, m in zip(shifts, shares)
            ]

        def swap(mine):
            return [permute_all(m, lambda r, c, p: (r, c ^ 1, p)) for m in mine]

        blocks = [((0, p * width), (pairs, width))]
        blocks += [share(s, 0, *span) for span in halves for s in shifts]
        blocks += [share(s, j, 0, width) for j in range(1, Q) for s in shifts]
        starts = [x for start, _ in blocks for x in start]
        places = jnp.stack([jnp.asarray(x, jnp.int32) for x in (p, core, jnp.where(r == c, 0, 1), *starts)])
        own, *shares = cut_out(places, slab, [shape for _, shape in blocks])
        shares = [shares[i : i + Q - 1] for i in range(0, len(shares), Q - 1)]

        other_weights = jnp.concatenate(
            [permute_all(weights, lambda r, c, p: (r, c, (p - s) % Q)) for s in shifts]
        )
        direct_own = send(own)
        pieces = []
        for (start, _), part in zip(halves, shares):
            received = exchange(part)
            pieces.append((start, received, swap(received)))
        mine = [array for _, received, _ in pieces for array in received]
        others = [assemble(places, pieces, *span) for span in spans]
        direct_others = [send(others[0])]
        rest = []
        for part in shares[len(halves) :]:
            part = hold(part, [(0, width)], other_weights)[0]
            for piece in hold(part, halves, *mine):
                received = exchange(piece)
                received = hold(received, [(0, received[0].shape[1])], direct_own)[0]
                rest.append((received, swap(received)))
        rows = weigh(places, slab, weights, others, rest, other_weights, width)
        for i, other in enumerate(others[1:], 1):
            earlier = rows if i == len(others) - 1 else direct_own
            direct_others.append(send(hold([other], [(0, other.shape[1])], earlier)[0][0]))
        result = None
        for other, sent, (start, _) in zip(others, direct_others, spans):
            result = product(places, rows, [own, direct_own], [other, sent], result, start, width)
        return result

    return jax.shard_map(
        on_device,
        mesh=mesh,
        in_specs=(P("pair", "row"), P("pair")),
        out_specs=P("row", ("col", "pair")),
        check_vma=False,
    )
```

```python
import jax
import jax.numpy as jnp
from jax import lax
from jax.experimental import pallas as pl
from jax.experimental.pallas import tpu as pltpu
from jax.sharding import PartitionSpec as P

AXES = ("row", "col", "pair")
LANES = 128
PLACE, CORE, OWN_OR_SENT, STARTS = range(4)
PARTS = 3
VMEM = pl.BlockSpec(memory_space=pltpu.VMEM)
SMEM = pl.BlockSpec(memory_space=pltpu.SMEM)
ANY = pl.BlockSpec(memory_space=pl.ANY)
HBM = pl.BlockSpec(memory_space=pltpu.HBM)


def params(mib):
    return pltpu.CompilerParams(vmem_limit_bytes=mib * 2**20)


def product(places, rows, own, other, result, first, columns):
    depth, height = rows.shape
    pairs, width = own[0].shape[0], other[0].shape[1]
    tile = 1024 if height % 1024 == 0 else height
    args = [places, rows, *own, *other]
    in_specs = [SMEM] + [VMEM] * (len(args) - 1)
    aliases = {}
    if result is not None:
        aliases = {len(args): 0}
        in_specs.append(ANY)
        args.append(result)

    def kernel(places, rows, *refs):
        out, held = refs[-2:]

        @pl.when(pl.program_id(0) == 0)
        def _():
            for part, choices in ((pl.ds(0, pairs), own), (pl.ds(pairs, depth - pairs), other)):
                skip = 0 if choices is own else len(own)
                for i in range(len(choices)):
                    start = first if choices is own else 0

                    @pl.when(places[OWN_OR_SENT] == i)
                    def _(part=part, i=skip + i, start=start):
                        held[part, :] = refs[i][:, start : start + width]

        at = pl.ds(pl.multiple_of(pl.program_id(0) * tile, tile), tile)
        out[...] = lax.dot_general(
            rows[:, at], held[...], (((0,), (0,)), ((), ())), preferred_element_type=jnp.float32
        )

    return pl.pallas_call(
        kernel,
        grid=(height // tile,),
        in_specs=in_specs,
        out_specs=pl.BlockSpec((pl.Element(tile), pl.Element(width)), lambda i: (i * tile, first)),
        out_shape=jax.ShapeDtypeStruct((height, columns), jnp.float32),
        scratch_shapes=[pltpu.VMEM((depth, width), jnp.bfloat16)],
        input_output_aliases=aliases,
        compiler_params=params(5 + (8 * tile + 2 * depth) * width // 2**20),
        cost_estimate=pl.CostEstimate(
            flops=2 * height * width * depth, bytes_accessed=4 * height * width, transcendentals=0
        ),
    )(*args)


def weigh(places, slab, weights, others, rest, other_weights, width):
    pairs, height = slab.shape
    half = pairs // 2
    shifts = len(rest[0][0])
    step = 64 if half % 64 == 0 else half
    arrays = [*others, *(m for mine, theirs in rest for m in (*mine, *theirs))]

    def kernel(places, slab, weights, other_weights, *refs):
        *refs, out, own, arrived = refs
        fetch = pltpu.make_async_copy(slab, own, arrived)
        fetch.start()

        def put(rows, by, ref, at, column):
            start = pl.multiple_of(lax.rem(places[PLACE] * width + column, height), LANES)
            to = pl.ds(pl.multiple_of(pairs + rows, step), step)
            value = by[pl.ds(pl.multiple_of(rows, step), step), :] * ref[at, :].astype(jnp.float32)
            out[to, pl.ds(start, ref.shape[1])] = value.astype(out.dtype)

        @pl.loop(0, shifts * pairs // step)
        def _(i):
            at = pl.ds(pl.multiple_of(i * step, step), step)
            column = 0
            for ref in refs[: len(others)]:
                put(i * step, other_weights, ref, at, column)
                column += ref.shape[1]

        @pl.loop(0, half // step)
        def _(i):
            at = pl.ds(pl.multiple_of(i * step, step), step)
            parts = iter(refs[len(others) :])
            column = width
            for mine, _ in rest:
                for first in (places[CORE], 1 - places[CORE]):
                    for shift in range(shifts):
                        put(shift * pairs + first * half + i * step, other_weights, next(parts), at, column)
                column += mine[0].shape[1]

        fetch.wait()

        @pl.loop(0, pairs // step)
        def _(i):
            at = pl.ds(pl.multiple_of(i * step, step), step)
            out[at, :] = (weights[at, :] * own[at, :].astype(jnp.float32)).astype(out.dtype)

    return pl.pallas_call(
        kernel,
        in_specs=[SMEM, HBM] + [VMEM] * (2 + len(arrays)),
        out_specs=VMEM,
        out_shape=jax.ShapeDtypeStruct(((1 + shifts) * pairs, height), slab.dtype),
        scratch_shapes=[pltpu.VMEM(slab.shape, slab.dtype), pltpu.SemaphoreType.DMA],
        compiler_params=params(3 + 2 * pairs * height // 2**20),
    )(places, slab, weights[:, None], other_weights[:, None], *arrays)


def split(width, count, last):
    lanes = (width - last) // LANES
    count = min(count, lanes)
    sizes = [LANES * (lanes // count + (i < lanes % count)) for i in range(count)] + [last] * (last > 0)
    return [(sum(sizes[:i]), size) for i, size in enumerate(sizes)]


def cut_out(places, slab, shapes):
    count = len(shapes)

    def kernel(places, slab, *refs):
        outs, done = refs[:count], refs[-1]
        copies = []
        for i, (rows, size) in enumerate(shapes):
            at = pl.ds(pl.multiple_of(places[STARTS + 2 * i], 16), rows)
            across = pl.ds(pl.multiple_of(places[STARTS + 2 * i + 1], LANES), size)
            copies.append(pltpu.make_async_copy(slab.at[at, across], outs[i], done.at[i]))
        for copy in copies:
            copy.start()
        for copy in copies:
            copy.wait()

    return pl.pallas_call(
        kernel,
        in_specs=[SMEM, HBM],
        out_specs=[VMEM] * count,
        out_shape=[jax.ShapeDtypeStruct(shape, slab.dtype) for shape in shapes],
        scratch_shapes=[pltpu.SemaphoreType.DMA((count,))],
        compiler_params=params(2),
    )(places, slab)


def assemble(places, pieces, start, size):
    count = len(pieces[0][1])
    half = pieces[0][1][0].shape[0]
    arrays = [array for _, mine, theirs in pieces for array in (*mine, *theirs)]

    def kernel(places, *refs):
        *refs, out = refs
        refs = iter(refs)
        for offset, mine, _ in pieces:
            low, high = max(start, offset), min(start + size, offset + mine[0].shape[1])
            for rows in (places[CORE], 1 - places[CORE]):
                for i in range(count):
                    ref = next(refs)
                    if low < high:
                        at = pl.ds(pl.multiple_of((2 * i + rows) * half, half), half)
                        out[at, low - start : high - start] = ref[:, low - offset : high - offset]

    return pl.pallas_call(
        kernel,
        in_specs=[SMEM] + [VMEM] * len(arrays),
        out_specs=VMEM,
        out_shape=jax.ShapeDtypeStruct((2 * count * half, size), arrays[0].dtype),
        compiler_params=params(2),
    )(places, *arrays)


def hold(values, spans, *earlier):
    count = len(values)

    def kernel(*refs):
        outs = iter(refs[count + len(earlier) :])
        for start, size in spans:
            for value in refs[:count]:
                next(outs)[...] = value[:, start : start + size]

    outs = pl.pallas_call(
        kernel,
        in_specs=[VMEM] * count + [ANY] * len(earlier),
        out_specs=[VMEM] * (count * len(spans)),
        out_shape=[jax.ShapeDtypeStruct((v.shape[0], n), v.dtype) for _, n in spans for v in values],
        compiler_params=params(2),
    )(*values, *earlier)
    return [outs[i : i + count] for i in range(0, len(outs), count)]


def pick_senders(planes, columns):
    per_side = columns // 2
    sends = [(b, t) for b in range(planes) for t in range(planes) if b != t]

    def cost(chosen):
        load, sources = {}, {}
        for (b, t), side in zip(sends, chosen):
            way = 1 if t > b else -1
            links = [(side, z, way) for z in range(b, t, way)]
            if side != b // per_side:
                links.append((t, side, "across"))
            for link in links:
                load[link] = load.get(link, 0) + 1
                sources.setdefault(link, set()).add(b)
        return sum(value**6 * (4 + len(sources[link])) for link, value in load.items())

    def full(chosen, i):
        return sum(s[0] == sends[i][0] and c == chosen[i] for s, c in zip(sends, chosen)) > per_side

    def settle(chosen):
        for i in sorted(range(len(sends)), key=lambda i: -abs(sends[i][0] - sends[i][1])):
            if full(chosen, i):
                chosen[i] = 1 - chosen[i]
        every = range(len(sends))
        best, better = cost(chosen), True
        while better:
            better = False
            for flips in [[i] for i in every] + [[i, j] for i in every for j in range(i)]:
                trial = list(chosen)
                for j in flips:
                    trial[j] = 1 - trial[j]
                if not any(full(trial, j) for j in flips) and cost(trial) < best:
                    chosen, best, better = trial, cost(trial), True
        return best, chosen

    def native(b, t):
        return b // per_side

    def apart(b, t):
        inward = t < b if b >= planes // 2 else t > b
        return 1 - native(b, t) if inward and (b not in (0, planes - 1) or abs(b - t) == 1) else native(b, t)

    starts = [[rule(*send) for send in sends] for rule in (native, apart)]
    _, chosen = min((settle(start) for start in starts), key=lambda result: result[0])
    result = {}
    for (b, t), side in zip(sends, chosen):
        used = [c for (x, _), c in result.items() if x == b]
        result[b, t] = [c for c in range(side * per_side, (side + 1) * per_side) if c not in used][0]
    return result


def solution(mesh):
    R, C, Q = (mesh.shape[axis] for axis in AXES)
    senders = pick_senders(R, C)

    def number(r, c, p):
        return (r * C + c) * Q + p

    def permute(block, moves):
        pairs = [(number(*source), number(*target)) for source, target in moves]
        return lax.ppermute(block, AXES, pairs) if pairs else jnp.zeros_like(block)

    def permute_all(block, route):
        every = [(r, c, p) for r in range(R) for c in range(C) for p in range(Q)]
        return permute(block, [(device, route(*device)) for device in every])

    def send(block):
        return permute(
            block, [((b, c, p), (t, b, p)) for (b, t), c in senders.items() for p in range(Q)]
        )

    def on_device(slab, weights):
        pairs, block = slab.shape
        width = block // Q
        spans = split(width, PARTS - 1, max(LANES, width * 3 // 16 // LANES * LANES))
        halves = split(width, 2, 0)
        shifts = range(1, Q)
        r, c, p = (lax.axis_index(axis) for axis in AXES)
        core = c % 2

        def share(shift, relative, offset, size):
            start = (p - shift + relative) % Q * width + offset
            return (core * (pairs // 2), start), (pairs // 2, size)

        def exchange(shares):
            return [
                permute_all(m, lambda r, c, p: (r, c, (p - s) % Q)) for s, m in zip(shifts, shares)
            ]

        def swap(mine):
            return [permute_all(m, lambda r, c, p: (r, c ^ 1, p)) for m in mine]

        blocks = [((0, p * width), (pairs, width))]
        blocks += [share(s, 0, *span) for span in halves for s in shifts]
        blocks += [share(s, j, 0, width) for j in range(1, Q) for s in shifts]
        starts = [x for start, _ in blocks for x in start]
        places = jnp.stack([jnp.asarray(x, jnp.int32) for x in (p, core, jnp.where(r == c, 0, 1), *starts)])
        own, *shares = cut_out(places, slab, [shape for _, shape in blocks])
        shares = [shares[i : i + Q - 1] for i in range(0, len(shares), Q - 1)]

        other_weights = jnp.concatenate(
            [permute_all(weights, lambda r, c, p: (r, c, (p - s) % Q)) for s in shifts]
        )
        direct_own = send(own)
        pieces = []
        for (start, _), part in zip(halves, shares):
            received = exchange(part)
            pieces.append((start, received, swap(received)))
        mine = [array for _, received, _ in pieces for array in received]
        others = [assemble(places, pieces, *span) for span in spans]
        direct_others = [send(others[0])]
        rest = []
        for part in shares[len(halves) :]:
            part = hold(part, [(0, width)], other_weights)[0]
            for piece in hold(part, halves, *mine):
                received = exchange(piece)
                received = hold(received, [(0, received[0].shape[1])], direct_own)[0]
                rest.append((received, swap(received)))
        rows = weigh(places, slab, weights, others, rest, other_weights, width)
        for i, other in enumerate(others[1:], 1):
            earlier = rows if i == len(others) - 1 else direct_own
            direct_others.append(send(hold([other], [(0, other.shape[1])], earlier)[0][0]))
        result = None
        for other, sent, (start, _) in zip(others, direct_others, spans):
            result = product(places, rows, [own, direct_own], [other, sent], result, start, width)
        return result

    return jax.shard_map(
        on_device,
        mesh=mesh,
        in_specs=(P("pair", "row"), P("pair")),
        out_specs=P("row", ("col", "pair")),
        check_vma=False,
    )
```
